256 devices in a mesh: section: 8 (over y, core), expert: 32 (over x, z).
Axes of the slice: x: 4, y: 4, z: 8, core: 2. Of those that a mesh axis runs over, the one named last changes fastest.
Arguments:
- down_tokens: bfloat16 [8, 2048, 7168], P('section', 'expert'), may hold values from -6 to 6
- up_tokens: bfloat16 [8, 2048, 7168], P('section', 'expert'), may hold values from -6 to 6
- down_routes: int32 [8, 2048, 1], P('section', 'expert'), may hold values from 0 to 3; in each aligned block of 64 rows (0 to 63, 64 to 127, ..., all dimensions but the last counted through in order) at most 32 rows name the same one
- up_routes: int32 [8, 2048, 1], P('section', 'expert'), may hold values from 0 to 3; in each aligned block of 64 rows (0 to 63, 64 to 127, ..., all dimensions but the last counted through in order) at most 32 rows name the same one
- down_gates: float32 [8, 2048, 1], P('section', 'expert'), may hold values from 0.3 to 2
- up_gates: float32 [8, 2048, 1], P('section', 'expert'), may hold values from 0.3 to 2
- w_gate: bfloat16 [8, 7168, 4096], P('section', None, 'expert'), may hold values from -0.0625 to 0.0625
- w_up: bfloat16 [8, 7168, 4096], P('section', None, 'expert'), may hold values from -0.0625 to 0.0625
- w_down: bfloat16 [8, 4096, 7168], P('section', 'expert'), may hold values from -0.1875 to 0.1875
Outputs:
- next_down: bfloat16 [8, 2048, 7168], P('section', 'expert')
- next_up: bfloat16 [8, 2048, 7168], P('section', 'expert')
The draws below stay inside these ranges and needn't reach their ends.
Inputs may be any that keep to these rules, and one draw needn't show every extreme that they name: `down_routes`: each row names 1 different experts. In every aligned block of 64 rows (the rows of one device), no expert is named more than 32 times, a bound that some block reaches. `up_routes`: as for down_routes.
All inputs are finite; a program needn't handle non-finite values.
Results may differ from the reference program's by a relative error of at most 0.01.
Values may be sent and summed in bfloat16 or wider, within the bound.
No kernel may reach another device: no remote copies, remote signals or barrier semaphores. Data moves between devices by JAX's collectives and lax.ppermute only.
A program may use at most 192 MiB of HBM per device.

```python
import math
import jax
import jax.numpy as jnp
import numpy as np
from jax import lax

D = 7168
HID = 1024
SPLIT = 8
TOP = 1
MB_TOK = 64
HID_DEV = 128
EXPERTS = 4
CAP = 32
TOKENS = 2048
N_SECTION = 8
N_EXPERT = 32


def shard_levels(rng, dims, split, least, high):
    def one(dim, shards_of):
        heights = jax.random.uniform(jax.random.fold_in(jax.random.fold_in(rng, 6), dim), (shards_of,), jnp.float32, least / len(split), high / len(split))
        return jnp.repeat(jnp.exp(heights), dims[dim] // shards_of).reshape((-1,) + (1,) * (len(dims) - dim - 1))

    level = one(*split[0])
    for cut in split[1:]:
        level = level * one(*cut)
    return level


def routed_block(own_key, own, number, rows, count, top, reach, slope):
    order = jax.random.permutation(own_key, count)
    heavy_load, usual = shares(count, rows * top, reach, slope, True), shares(count, rows * top, reach, slope, False)
    places = jnp.arange(count)

    def named(lengths, offset_by):
        used = int((lengths > 0).sum())
        fixed = max(1, used // 4)
        moved = fixed + (places - fixed + offset_by * (used - fixed)) % max(1, count - fixed)
        return jnp.zeros((count,), jnp.int32).at[order[jnp.where(places < fixed, places, moved)]].set(jnp.asarray(lengths, jnp.int32))

    lengths = jnp.where(number % 4 == 0, named(heavy_load, number // 4), named(usual, number - number // 4 - 1))
    mixed = jax.random.permutation(jax.random.fold_in(own, 3), count)
    giver, taker = mixed[0:count // 2 * 2:2], mixed[1:count // 2 * 2:2]
    margin = jnp.minimum(lengths[giver] - 1, reach - lengths[taker]) // 2
    margin = jnp.where((giver == order[0]) | (taker == order[0]) | (lengths[taker] == 0), 0, jnp.maximum(margin, 0))
    moved = jax.random.randint(jax.random.fold_in(own, 4), (count // 2,), 0, 1 << 20) % (margin + 1)
    lengths = lengths.at[giver].add(-moved).at[taker].add(moved)
    members = jnp.searchsorted(jnp.cumsum(lengths), jnp.arange(rows * top), side="right").astype(jnp.int32)
    grid = members.reshape(top, rows).T
    grid = grid[jax.random.permutation(jax.random.fold_in(own, 1), rows)]
    offset_by = jax.random.randint(jax.random.fold_in(own, 2), (rows, 1), 0, top)
    return jnp.take_along_axis(grid, (jnp.arange(top)[None, :] + offset_by) % top, axis=1)


def shares(number_of, total, most, slope, full):
    weights = [(1 << 20) // math.isqrt(rank ** slope) + 1 for rank in range(1, number_of + 1)]
    largest = most if full else min(most, max(-(-total // number_of), total * weights[0] // sum(weights)))
    least = 1 if total - largest >= number_of - 1 else 0
    counts, rest = [largest] + [least] * (number_of - 1), total - largest - least * (number_of - 1)
    while rest > 0:
        movable = [i for i in range(1, number_of) if counts[i] < largest] or [i for i in range(1, number_of) if counts[i] < most]
        whole, left = sum([weights[i] for i in movable]), rest
        for i in movable:
            extra = min(most - counts[i], max(1, left * weights[i] // whole), rest)
            counts[i] = counts[i] + extra
            rest = rest - extra
    return np.array(counts)


def normal_values(stream_key, shape, spread, reach, split=(), kind=jnp.bfloat16):
    entries = spread * jax.random.normal(stream_key, shape, jnp.float32)
    if split:
        entries = entries * shard_levels(stream_key, shape, split, -0.22, 0.18)
    return jnp.clip(entries, -reach, reach).astype(kind)


def setup_inputs(seed: int = 0) -> dict:
    seeds = jax.random.split(jax.random.key(seed), 10)
    down_tokens = normal_values(seeds[0], (N_SECTION, TOKENS, D), 1.0, 6.0, ((0, 8), (1, 32)))
    up_tokens = normal_values(seeds[1], (N_SECTION, TOKENS, D), 1.0, 6.0, ((0, 8), (1, 32)))
    down_routes_keys = jax.random.split(jax.random.fold_in(seeds[2], 1), N_SECTION * TOKENS // MB_TOK)
    down_routes_turns = jax.random.permutation(jax.random.fold_in(seeds[2], 3), N_SECTION * TOKENS // MB_TOK)
    down_routes = jax.vmap(lambda own, number: routed_block(jax.random.fold_in(seeds[2], 2), own, number, MB_TOK, EXPERTS, TOP, CAP, 2))(down_routes_keys, down_routes_turns).reshape((N_SECTION, TOKENS, TOP))
    up_routes_keys = jax.random.split(jax.random.fold_in(seeds[3], 1), N_SECTION * TOKENS // MB_TOK)
    up_routes_turns = jax.random.permutation(jax.random.fold_in(seeds[3], 3), N_SECTION * TOKENS // MB_TOK)
    up_routes = jax.vmap(lambda own, number: routed_block(jax.random.fold_in(seeds[3], 2), own, number, MB_TOK, EXPERTS, TOP, CAP, 2))(up_routes_keys, up_routes_turns).reshape((N_SECTION, TOKENS, TOP))
    down_gates = jnp.clip(jnp.exp(math.log(2.0) - 1.89712 * jax.random.uniform(seeds[4], (N_SECTION, TOKENS, TOP), jnp.float32) ** shard_levels(seeds[4], (N_SECTION, TOKENS, TOP), ((0, 8), (1, 32)), -0.2, 0.2)), 0.3, 2.0)
    up_gates = jnp.clip(jnp.exp(math.log(2.0) - 1.89712 * jax.random.uniform(seeds[5], (N_SECTION, TOKENS, TOP), jnp.float32) ** shard_levels(seeds[5], (N_SECTION, TOKENS, TOP), ((0, 8), (1, 32)), -0.2, 0.2)), 0.3, 2.0)
    w_gate = normal_values(seeds[6], (N_SECTION, D, EXPERTS * HID), D ** -0.5, 0.0625, ((0, 8), (2, 32)))
    w_up = normal_values(seeds[7], (N_SECTION, D, EXPERTS * HID), D ** -0.5, 0.0625, ((0, 8), (2, 32)))
    w_down = normal_values(seeds[8], (N_SECTION, EXPERTS * HID, D), HID ** -0.5, 0.1875, ((0, 8), (1, 32)))
    return {"down_tokens": down_tokens, "up_tokens": up_tokens, "down_routes": down_routes, "up_routes": up_routes, "down_gates": down_gates, "up_gates": up_gates, "w_gate": w_gate, "w_up": w_up, "w_down": w_down}


def build_buffer(block_tokens, block_routes):
    rows = block_tokens.shape[0]
    one_hot = (block_routes[:, :, None] == jnp.arange(EXPERTS, dtype=jnp.int32)[None, None, :]).astype(jnp.int32)
    flat = one_hot.reshape(rows * TOP, EXPERTS)
    before = jnp.cumsum(flat, axis=0) - flat
    slot = jnp.sum(before * flat, axis=1).reshape(rows, TOP)
    target = (block_routes * CAP + slot).astype(jnp.int32)
    select = (target.reshape(-1)[None, :] == jnp.arange(EXPERTS * CAP, dtype=jnp.int32)[:, None]).astype(jnp.bfloat16)
    repeated = jnp.repeat(block_tokens, TOP, axis=0)
    buffer = jnp.dot(select, repeated, preferred_element_type=jnp.float32).astype(jnp.bfloat16)
    return buffer.reshape(EXPERTS, CAP, D), target


def one_path(tokens, routes, gates, w_gate, w_up, w_down):
    blocks = tokens.reshape(N_EXPERT, MB_TOK, D)
    block_routes = routes.reshape(N_EXPERT, MB_TOK, TOP)
    buffers, targets = jax.vmap(build_buffer)(blocks, block_routes)

    def per_expert(e):
        start = (e * HID).astype(jnp.int32)
        rows = buffers[:, e].reshape(N_EXPERT * CAP, D)
        wg = lax.dynamic_slice_in_dim(w_gate, start, HID, 1)
        wu = lax.dynamic_slice_in_dim(w_up, start, HID, 1)
        wd = lax.dynamic_slice_in_dim(w_down, start, HID, 0)
        gate = jnp.dot(rows, wg, preferred_element_type=jnp.float32)
        up = jnp.dot(rows, wu, preferred_element_type=jnp.float32)
        hidden = (jax.nn.silu(gate) * up).astype(jnp.bfloat16)
        hidden_split = hidden.reshape(N_EXPERT * CAP, SPLIT, HID_DEV).astype(jnp.float32)
        down_split = wd.reshape(SPLIT, HID_DEV, D).astype(jnp.float32)
        parts = jnp.einsum("rjh,jhd->jrd", hidden_split, down_split, precision=lax.Precision.HIGHEST).astype(jnp.bfloat16)
        total = jnp.sum(parts.astype(jnp.float32), axis=0)
        return total.reshape(N_EXPERT, CAP, D)

    values = lax.map(per_expert, jnp.arange(EXPERTS, dtype=jnp.int32))
    values = jnp.transpose(values, (1, 0, 2, 3)).reshape(N_EXPERT, EXPERTS * CAP, D)

    def combine(block, vals, target, gate_block):
        picked = jnp.take(vals, target.reshape(-1), axis=0).reshape(MB_TOK, TOP, D)
        mixed = jnp.sum(picked * gate_block[:, :, None], axis=1)
        return (block.astype(jnp.float32) + mixed).astype(jnp.bfloat16)

    outputs = jax.vmap(combine)(blocks, values, targets, gates.reshape(N_EXPERT, MB_TOK, TOP))
    return outputs.reshape(TOKENS, D)


def reference(down_tokens, up_tokens, down_routes, up_routes, down_gates, up_gates, w_gate, w_up, w_down):
    def per_section(items):
        d_tok, u_tok, d_rt, u_rt, d_gt, u_gt, wg, wu, wd = items
        y_down = one_path(d_tok, d_rt, d_gt, wg, wu, wd)
        y_up = one_path(u_tok, u_rt, u_gt, wg, wu, wd)
        return y_down, y_up

    y_down, y_up = lax.map(per_section, (down_tokens, up_tokens, down_routes, up_routes, down_gates, up_gates, w_gate, w_up, w_down))
    next_down = jnp.concatenate([y_up[:1], y_down[:-1]], axis=0)
    next_up = jnp.concatenate([y_up[1:], y_down[-1:]], axis=0)
    return next_down, next_up
```

```python
import jax
import jax.numpy as jnp
from jax import lax
from jax.sharding import Mesh, PartitionSpec as P

SPLIT = 8


def shifted(block, axis, distance):
    n = lax.axis_size(axis)
    return lax.ppermute(block, axis, [(i, (i + distance) % n) for i in range(n)])


def passed_along(block, axis, distance):
    devices = range(lax.axis_size(axis))
    route = [(i - distance, i) for i in devices if i - distance in devices]
    return lax.ppermute(block, axis, route)


def gathered_along_x(block):
    half = block.shape[0] // 2
    before = shifted(block, "x", 1)
    after = shifted(block, "x", -1)
    top = shifted(before[:half], "x", 1)
    bottom = shifted(after[half:], "x", -1)
    return [(0, block), (-1, before), (1, after), (2, (top, bottom))]


def product(rows, block):
    if isinstance(block, tuple):
        half = block[0].shape[0]
        return product(rows[:, :half], block[0]) + product(rows[:, half:], block[1])
    return jnp.dot(rows, block, preferred_element_type=jnp.float32)


def body(
    down_tokens, up_tokens, down_routes, up_routes, down_gates, up_gates, w_gate, w_up, w_down
):
    n_x, n_z = lax.axis_size("x"), lax.axis_size("z")
    me_x = lax.axis_index("x")
    rows, width = down_tokens.shape[1:]
    part = width // n_z
    hid = w_gate.shape[2]
    tokens = (down_tokens[0], up_tokens[0])
    gates = (down_gates[0], up_gates[0])

    routes = lax.all_gather(
        jnp.concatenate([down_routes[0], up_routes[0]], axis=1), "z"
    )
    routes = routes.reshape(n_z * rows, 2)

    w_down_cut = lax.all_to_all(
        w_down[0].reshape(hid, n_z, part).transpose(1, 0, 2), "z", 0, 0
    ).reshape(n_z * hid, part)
    gate_up = gathered_along_x(jnp.concatenate([w_gate[0], w_up[0]], axis=1))
    down = gathered_along_x(w_down_cut)

    results = []
    for p in range(2):
        mine = routes[:, p : p + 1]
        x = lax.all_gather(tokens[p], "z").reshape(n_z * rows, width)
        chosen = None
        for offset, block in gate_up:
            value = product(x, block)
            here = mine == (me_x + offset + n_x) % n_x
            chosen = value if chosen is None else jnp.where(here, value, chosen)
        hidden = (jax.nn.silu(chosen[:, :hid]) * chosen[:, hid:]).astype(jnp.bfloat16)
        hidden = lax.all_gather(hidden, "z", axis=1, tiled=True)
        out = None
        for offset, block in down:
            here = mine == (me_x + offset + n_x) % n_x
            term = product(jnp.where(here, hidden, jnp.zeros_like(hidden)), block)
            out = term if out is None else out + term
        out = out.astype(jnp.bfloat16).reshape(n_z, rows, part)
        out = lax.all_to_all(out, "z", 0, 0)
        out = out.transpose(1, 0, 2).reshape(rows, width)
        y = tokens[p].astype(jnp.float32) + gates[p] * out.astype(jnp.float32)
        results.append(y.astype(jnp.bfloat16))

    y_down, y_up = results
    section = lax.axis_index("section")
    last = lax.axis_size("section") - 1
    next_down = jnp.where(section == 0, y_up, passed_along(y_down, "section", 1))
    next_up = jnp.where(section == last, y_down, passed_along(y_up, "section", -1))
    return next_down[None], next_up[None]


def solution(mesh):
    sections, devices = mesh.devices.shape
    fine = Mesh(mesh.devices.reshape(sections, devices // SPLIT, SPLIT), ("section", "x", "z"))
    by_rows = P("section", ("x", "z"), None)
    by_columns = P("section", None, ("x", "z"))
    return jax.shard_map(
        body,
        mesh=fine,
        in_specs=(by_rows,) * 6 + (by_columns, by_columns, by_rows),
        out_specs=(by_rows, by_rows),
        check_vma=False,
    )
```

```python
import functools

import jax
import jax.numpy as jnp
from jax import lax
from jax.experimental import pallas as pl
from jax.experimental.pallas import tpu as pltpu
from jax.sharding import Mesh, PartitionSpec as P

SPLIT = 8
VMEM_BYTES = 60 * 1024 * 1024


def shifted(block, axis, distance):
    n = lax.axis_size(axis)
    return lax.ppermute(block, axis, [(i, (i + distance) % n) for i in range(n)])


class Order:
    def __init__(self, mark):
        self.mark = mark

    def __call__(self, *values):
        self.mark, *values = lax.optimization_barrier((self.mark, *values))
        return values


class Ring:
    def __init__(self, block, axis):
        self.axis, self.n, self.step = axis, lax.axis_size(axis), 0
        self.last = (block, block)
        self.up, self.down = [block], []

    def send(self):
        up, down = self.last
        self.step += 1
        if self.step == self.n // 2:
            half = up.shape[0] // 2
            up, down = up[:half], down[half:]
        self.last = (shifted(up, self.axis, -1), shifted(down, self.axis, 1))

    def wait(self, order, *others):
        self.last, *others = order(self.last, *others)
        if self.step < self.n // 2:
            self.up.append(self.last[0])
            self.down.insert(0, self.last[1])
        return others

    def near(self):
        return self.up + self.down


def hidden_kernel(n_rows, *refs):
    rows, tails, weights = refs[:n_rows], refs[n_rows : 2 * n_rows], refs[2 * n_rows]
    hidden, route, total = refs[-3:]
    n_experts, _, pair = weights.shape
    n_hid = pair // 2
    step = pl.program_id(0)

    def joined(blocks):
        blocks = [r[...] for r in blocks]
        return blocks[0] if len(blocks) == 1 else jnp.concatenate(blocks, axis=0)

    @pl.when(step == 0)
    def _():
        total[...] = jnp.zeros_like(total)
        route[...] = joined(tails)

    x = joined(rows)
    for e in range(n_experts):
        at = slice(pair * e, pair * (e + 1))
        total[:, at] += jnp.dot(x, weights[e], preferred_element_type=jnp.float32)

    @pl.when(step == pl.num_programs(0) - 1)
    def _():
        named = route[...].astype(jnp.float32)
        gate, up = total[:, :n_hid], total[:, n_hid:pair]
        for e in range(1, n_experts):
            here, at = named == e, pair * e
            gate = jnp.where(here, total[:, at : at + n_hid], gate)
            up = jnp.where(here, total[:, at + n_hid : at + pair], up)
        hidden[...] = (gate / (1.0 + jnp.exp(-gate)) * up).astype(hidden.dtype)


def hidden_of(rows, weights, block):
    n_experts, width, pair = weights.shape
    n_hid = pair // 2
    count = sum(r.shape[0] for r in rows)
    made = jax.ShapeDtypeStruct((count, n_hid), jnp.bfloat16)
    return pl.pallas_call(
        functools.partial(hidden_kernel, len(rows)),
        grid=(width // block,),
        in_specs=[pl.BlockSpec((r.shape[0], block), lambda k: (0, k)) for r in rows]
        + [pl.BlockSpec((r.shape[0], n_hid), lambda k: (0, width // n_hid)) for r in rows]
        + [pl.BlockSpec((n_experts, block, pair), lambda k: (0, k, 0))],
        out_specs=[pl.BlockSpec((count, n_hid), lambda k: (0, 0))] * 2,
        out_shape=[made, made],
        scratch_shapes=[pltpu.VMEM((count, pair * n_experts), jnp.float32)],
        compiler_params=pltpu.CompilerParams(
            dimension_semantics=("arbitrary",), vmem_limit_bytes=VMEM_BYTES
        ),
        cost_estimate=pl.CostEstimate(
            flops=2 * count * width * pair * n_experts,
            bytes_accessed=2 * width * (count + pair * n_experts),
            transcendentals=count * n_hid,
        ),
    )(*rows, *rows, weights)


def out_kernel(n_experts, slices, route, *refs):
    hidden, weights = refs[:slices], refs[slices : slices + 2]
    out, total = refs[-2:]
    step = pl.program_id(0)
    named = route[...].astype(jnp.float32)

    @pl.when(step == 0)
    def _():
        total[...] = jnp.zeros_like(total)

    for now in range(slices // 2):

        @pl.when(step == now)
        def _():
            sums = total[...]
            for half, weight in zip((hidden[now], hidden[now + slices // 2]), weights):
                terms = [jnp.where(named == e, half[...], jnp.zeros_like(half)) for e in range(n_experts)]
                sums += jnp.dot(
                    jnp.concatenate(terms, axis=1),
                    weight[...].reshape(-1, weight.shape[2]),
                    preferred_element_type=jnp.float32,
                )
            total[...] = sums

    @pl.when(step == pl.num_programs(0) - 1)
    def _():
        out[...] = total[...].astype(out.dtype)


def out_of(route, hidden, weights):
    slices = len(hidden)
    n_experts, _, part = weights.shape
    count, n_hid = route.shape
    steps = slices // 2
    return pl.pallas_call(
        functools.partial(out_kernel, n_experts, slices),
        grid=(steps,),
        in_specs=[pl.BlockSpec((count, n_hid), lambda k: (0, 0))]
        + [pl.BlockSpec((count, n_hid), lambda k, at=at: (at, 0)) for _, at in hidden]
        + [pl.BlockSpec((n_experts, n_hid, part), lambda k: (0, k, 0))]
        + [pl.BlockSpec((n_experts, n_hid, part), lambda k: (0, k + steps, 0))],
        out_specs=pl.BlockSpec((count, part), lambda k: (0, 0)),
        out_shape=jax.ShapeDtypeStruct((count, part), jnp.bfloat16),
        scratch_shapes=[pltpu.VMEM((count, part), jnp.float32)],
        compiler_params=pltpu.CompilerParams(
            dimension_semantics=("arbitrary",), vmem_limit_bytes=VMEM_BYTES
        ),
        cost_estimate=pl.CostEstimate(
            flops=2 * count * slices * n_hid * n_experts * part,
            bytes_accessed=2 * slices * n_hid * (count + n_experts * part),
            transcendentals=0,
        ),
    )(route, *[h for h, _ in hidden], weights, weights)


def body(
    down_tokens, up_tokens, down_routes, up_routes, down_gates, up_gates, w_gate, w_up, w_down
):
    n_x, n_z = lax.axis_size("x"), lax.axis_size("z")
    me_x, me_z = lax.axis_index("x"), lax.axis_index("z")
    section = lax.axis_index("section")
    sections = lax.axis_size("section")
    even = section % 2 == 0
    rows, width = down_tokens.shape[1:]
    part = width // n_z
    hid = w_gate.shape[2]

    def streams(down, up):
        return jnp.where(even, up, down), jnp.where(even, down, up)

    tokens = streams(down_tokens[0], up_tokens[0])
    gates = streams(down_gates[0], up_gates[0])
    routes = streams(down_routes[0], up_routes[0])

    def marked(s):
        route = jnp.broadcast_to(routes[s].astype(jnp.bfloat16), (rows, hid))
        return jnp.concatenate([tokens[s], route], axis=1)

    def by_place(near, far, s):
        near = near.reshape(2, n_z - 1, rows, hid)[s]
        far = far.reshape(2, 1, rows, hid)[s]
        turned = jnp.concatenate([near[: n_z // 2], far, near[n_z // 2 :]], axis=0)
        return jnp.roll(turned, me_z, axis=0).reshape(-1, hid)

    def finished(s, out):
        out = out.transpose(1, 0, 2).reshape(rows, width)
        y = tokens[s].astype(jnp.float32) + gates[s] * out.astype(jnp.float32)
        return y.astype(jnp.bfloat16)

    order = Order(gates[0])
    gate_up = lax.all_gather(jnp.concatenate([w_gate[0], w_up[0]], axis=1), "x")
    b, a = Ring(marked(0), "z"), Ring(marked(1), "z")
    b.send()
    a.send()
    w_cut = w_down[0].reshape(hid, n_z, part).transpose(1, 0, 2)
    w_cut = lax.all_to_all(w_cut, "z", 0, 0)
    b.wait(order)
    b.send()
    a.wait(order)
    a.send()
    (w_cut,) = b.wait(order, w_cut)
    b.send()
    w_cut = jnp.roll(w_cut, -me_z, axis=0).reshape(n_z * hid, part)
    a.wait(order)
    a.send()
    b.wait(order)
    b.send()
    a.wait(order)
    a.send()
    down = lax.all_gather(w_cut, "x")
    near = jnp.concatenate(b.near() + a.near(), axis=0)
    near, near_route = hidden_of([near], gate_up, 1024)
    (near,) = b.wait(order, near)
    a.wait(order)
    far, far_route = hidden_of(b.last + a.last, gate_up, 1024)
    both = jnp.concatenate([by_place(near, far, s) for s in range(2)], axis=0)
    named = [by_place(near_route, far_route, s) for s in range(2)]
    h = Ring(both, "z")
    h.send()
    h.wait(order)
    h.send()
    h.wait(order)
    h.send()
    h.wait(order)
    h.send()
    h.wait(order)
    (down,) = order(down)

    def out_rows(s):
        hidden = [(piece, s) for piece in h.up] + [(h.last[s], 0)] + [(piece, s) for piece in h.down]
        return out_of(named[s], hidden, down).reshape(n_z, rows, part)

    out_b = lax.all_to_all(out_rows(0), "z", 0, 0)
    out_b, out_a = order(out_b, out_rows(1))
    out_a = lax.all_to_all(out_a, "z", 0, 0)
    gates = (order.mark, gates[1])
    results = [finished(0, out_b), finished(1, out_a)]

    near = [(i, i ^ 1) for i in range(sections)]
    away = [(i, min(max(((i + 1) ^ 1) - 1, 0), sections - 1)) for i in range(sections)]
    from_away = lax.ppermute(results[0], "section", away)
    from_near = lax.ppermute(results[1], "section", near)
    next_down = jnp.where(even, from_away, from_near)
    next_up = jnp.where(even, from_near, from_away)
    return next_down[None], next_up[None]


def solution(mesh):
    sections, devices = mesh.devices.shape
    fine = Mesh(mesh.devices.reshape(sections, devices // SPLIT, SPLIT), ("section", "x", "z"))
    by_rows = P("section", ("x", "z"), None)
    by_columns = P("section", None, ("x", "z"))
    return jax.shard_map(
        body,
        mesh=fine,
        in_specs=(by_rows,) * 6 + (by_columns, by_columns, by_rows),
        out_specs=(by_rows, by_rows),
        check_vma=False,
    )
```

```python
import functools

import jax
import jax.numpy as jnp
from jax import lax
from jax.experimental import pallas as pl
from jax.experimental.pallas import tpu as pltpu
from jax.sharding import Mesh, PartitionSpec as P

SPLIT = 8
VMEM_BYTES = 60 * 1024 * 1024


def shifted(block, axis, distance):
    n = lax.axis_size(axis)
    return lax.ppermute(block, axis, [(i, (i + distance) % n) for i in range(n)])


class Order:
    def __init__(self, mark):
        self.mark = mark

    def __call__(self, *values):
        self.mark, *values = lax.optimization_barrier((self.mark, *values))
        return values


class Ring:
    def __init__(self, block, axis):
        self.axis, self.n, self.step = axis, lax.axis_size(axis), 0
        self.last = (block, block)
        self.up, self.down = [block], []

    def send(self):
        up, down = self.last
        self.step += 1
        if self.step == self.n // 2:
            half = up.shape[0] // 2
            up, down = up[:half], down[half:]
        self.last = (shifted(up, self.axis, -1), shifted(down, self.axis, 1))

    def wait(self, order, *others):
        self.last, *others = order(self.last, *others)
        if self.step < self.n // 2:
            self.up.append(self.last[0])
            self.down.insert(0, self.last[1])
        return others

    def near(self):
        return self.up + self.down


def hidden_kernel(n_rows, *refs):
    rows, tails = refs[:n_rows], refs[n_rows : 2 * n_rows]
    weights = refs[2 * n_rows : -3]
    hidden, route, total = refs[-3:]
    n_experts, n_hid = len(weights) // 2, hidden.shape[1]
    step = pl.program_id(0)

    @pl.when(step == 0)
    def _():
        total[...] = jnp.zeros_like(total)
        route[...] = jnp.concatenate([r[...] for r in tails], axis=0)

    x = jnp.concatenate([r[...] for r in rows], axis=0)
    for e in range(n_experts):
        at = slice(2 * n_hid * e, 2 * n_hid * (e + 1))
        pair = jnp.concatenate([weights[2 * e][0], weights[2 * e + 1][0]], axis=1)
        total[:, at] += jnp.dot(x, pair, preferred_element_type=jnp.float32)

    @pl.when(step == pl.num_programs(0) - 1)
    def _():
        named = route[...].astype(jnp.float32)
        gate, up = total[:, :n_hid], total[:, n_hid : 2 * n_hid]
        for e in range(1, n_experts):
            here, at = named == e, 2 * n_hid * e
            gate = jnp.where(here, total[:, at : at + n_hid], gate)
            up = jnp.where(here, total[:, at + n_hid : at + 2 * n_hid], up)
        hidden[...] = (gate / (1.0 + jnp.exp(-gate)) * up).astype(hidden.dtype)


def hidden_of(rows, gates, ups, block):
    n_experts, width, n_hid = gates.shape
    count = sum(r.shape[0] for r in rows)
    made = jax.ShapeDtypeStruct((count, n_hid), jnp.bfloat16)
    return pl.pallas_call(
        functools.partial(hidden_kernel, len(rows)),
        grid=(width // block,),
        in_specs=[pl.BlockSpec((r.shape[0], block), lambda k: (0, k)) for r in rows]
        + [pl.BlockSpec((r.shape[0], n_hid), lambda k: (0, width // n_hid)) for r in rows]
        + [pl.BlockSpec((1, block, n_hid), lambda k, e=e: (e, k, 0)) for e in range(n_experts) for _ in range(2)],
        out_specs=[pl.BlockSpec((count, n_hid), lambda k: (0, 0))] * 2,
        out_shape=[made, made],
        scratch_shapes=[pltpu.VMEM((count, 2 * n_hid * n_experts), jnp.float32)],
        compiler_params=pltpu.CompilerParams(
            dimension_semantics=("arbitrary",), vmem_limit_bytes=VMEM_BYTES
        ),
        cost_estimate=pl.CostEstimate(
            flops=4 * count * width * n_hid * n_experts,
            bytes_accessed=2 * width * (count + 2 * n_hid * n_experts),
            transcendentals=count * n_hid,
        ),
    )(*rows, *rows, *[gates, ups] * n_experts)


def out_kernel(n_experts, slices, route, *refs):
    hidden, weights = refs[:slices], refs[slices:-2]
    out, total = refs[-2:]
    step = pl.program_id(0)
    named = route[...].astype(jnp.float32)

    @pl.when(step == 0)
    def _():
        total[...] = jnp.zeros_like(total)

    for now in range(slices // 2):

        @pl.when(step == now)
        def _():
            sums = total[...]
            for at, half in enumerate((hidden[now], hidden[now + slices // 2])):
                terms = [jnp.where(named == e, half[...], jnp.zeros_like(half)) for e in range(n_experts)]
                sums += jnp.dot(
                    jnp.concatenate(terms, axis=1),
                    jnp.concatenate([weights[2 * e + at][0] for e in range(n_experts)], axis=0),
                    preferred_element_type=jnp.float32,
                )
            total[...] = sums

    @pl.when(step == pl.num_programs(0) - 1)
    def _():
        out[...] = total[...].astype(out.dtype)


def out_of(route, hidden, weights):
    slices = len(hidden)
    n_experts, _, part = weights.shape
    count, n_hid = route.shape
    steps = slices // 2
    return pl.pallas_call(
        functools.partial(out_kernel, n_experts, slices),
        grid=(steps,),
        in_specs=[pl.BlockSpec((count, n_hid), lambda k: (0, 0))]
        + [pl.BlockSpec((count, n_hid), lambda k, at=at: (at, 0)) for _, at in hidden]
        + [
            pl.BlockSpec((1, n_hid, part), lambda k, e=e, at=at: (e, k + at, 0))
            for e in range(n_experts)
            for at in (0, steps)
        ],
        out_specs=pl.BlockSpec((count, part), lambda k: (0, 0)),
        out_shape=jax.ShapeDtypeStruct((count, part), jnp.bfloat16),
        scratch_shapes=[pltpu.VMEM((count, part), jnp.float32)],
        compiler_params=pltpu.CompilerParams(
            dimension_semantics=("arbitrary",), vmem_limit_bytes=VMEM_BYTES
        ),
        cost_estimate=pl.CostEstimate(
            flops=2 * count * slices * n_hid * n_experts * part,
            bytes_accessed=2 * slices * n_hid * (count + n_experts * part),
            transcendentals=0,
        ),
    )(route, *[h for h, _ in hidden], *[weights] * (2 * n_experts))


def body(
    down_tokens, up_tokens, down_routes, up_routes, down_gates, up_gates, w_gate, w_up, w_down
):
    n_x, n_z = lax.axis_size("x"), lax.axis_size("z")
    me_x, me_z = lax.axis_index("x"), lax.axis_index("z")
    section = lax.axis_index("section")
    sections = lax.axis_size("section")
    even = section % 2 == 0
    rows, width = down_tokens.shape[1:]
    part = width // n_z
    hid = w_gate.shape[2]

    def streams(down, up):
        return jnp.where(even, up, down), jnp.where(even, down, up)

    tokens = streams(down_tokens[0], up_tokens[0])
    gates = streams(down_gates[0], up_gates[0])
    routes = streams(down_routes[0], up_routes[0])

    def marked(s):
        route = jnp.broadcast_to(routes[s].astype(jnp.bfloat16), (rows, hid))
        return jnp.concatenate([tokens[s], route], axis=1)

    def by_place(first, second, s):
        n_first = 2 * (n_z // 2 - 2) + 1
        first = first.reshape(2, n_first, rows, hid)[s]
        second = second.reshape(2, n_z - n_first, rows, hid)[s]
        keep = (n_first + 1) // 2
        turned = jnp.concatenate([first[:keep], second, first[keep:]], axis=0)
        return jnp.roll(turned, me_z, axis=0).reshape(-1, hid)

    def finished(s, out):
        out = out.transpose(1, 0, 2).reshape(rows, width)
        y = tokens[s].astype(jnp.float32) + gates[s] * out.astype(jnp.float32)
        return y.astype(jnp.bfloat16)

    order = Order(gates[0])
    gate_all = lax.all_gather(w_gate[0], "x")
    up_all = lax.all_gather(w_up[0], "x")
    b, a = Ring(marked(0), "z"), Ring(marked(1), "z")
    b.send()
    a.send()
    w_cut = w_down[0].reshape(hid, n_z, part).transpose(1, 0, 2)
    w_cut = lax.all_to_all(w_cut, "z", 0, 0)
    b.wait(order)
    b.send()
    a.wait(order)
    a.send()
    (w_cut,) = b.wait(order, w_cut)
    b.send()
    w_cut = jnp.roll(w_cut, -me_z, axis=0).reshape(n_z * hid, part)
    down = lax.all_gather(w_cut, "x")
    a.wait(order)
    first = b.near() + a.near()
    a.send()
    b.wait(order)
    b.send()
    first, first_route = hidden_of(first, gate_all, up_all, 1792)
    (first,) = a.wait(order, first)
    a.send()
    b.wait(order)
    a.wait(order)
    second = [p for ring in (b, a) for p in (ring.up[-1], *ring.last, ring.down[0])]
    second, second_route = hidden_of(second, gate_all, up_all, 1792)
    both = jnp.concatenate([by_place(first, second, s) for s in range(2)], axis=0)
    named = [by_place(first_route, second_route, s) for s in range(2)]
    h = Ring(both, "z")
    h.send()
    h.wait(order)
    h.send()
    h.wait(order)
    h.send()
    h.wait(order)
    h.send()
    h.wait(order)
    (down,) = order(down)

    def out_rows(s):
        hidden = [(piece, s) for piece in h.up] + [(h.last[s], 0)] + [(piece, s) for piece in h.down]
        return out_of(named[s], hidden, down).reshape(n_z, rows, part)

    out_b = lax.all_to_all(out_rows(0), "z", 0, 0)
    out_b, out_a = order(out_b, out_rows(1))
    out_a = lax.all_to_all(out_a, "z", 0, 0)
    gates = (order.mark, gates[1])
    results = [finished(0, out_b), finished(1, out_a)]

    near = [(i, i ^ 1) for i in range(sections)]
    away = [(i, min(max(((i + 1) ^ 1) - 1, 0), sections - 1)) for i in range(sections)]
    from_away = lax.ppermute(results[0], "section", away)
    from_near = lax.ppermute(results[1], "section", near)
    next_down = jnp.where(even, from_away, from_near)
    next_up = jnp.where(even, from_near, from_away)
    return next_down[None], next_up[None]


def solution(mesh):
    sections, devices = mesh.devices.shape
    fine = Mesh(mesh.devices.reshape(sections, devices // SPLIT, SPLIT), ("section", "x", "z"))
    by_rows = P("section", ("x", "z"), None)
    by_columns = P("section", None, ("x", "z"))
    return jax.shard_map(
        body,
        mesh=fine,
        in_specs=(by_rows,) * 6 + (by_columns, by_columns, by_rows),
        out_specs=(by_rows, by_rows),
        check_vma=False,
    )
```

```python
import functools

import jax
import jax.numpy as jnp
from jax import lax
from jax.experimental import pallas as pl
from jax.experimental.pallas import tpu as pltpu
from jax.sharding import Mesh, PartitionSpec as P

SPLIT = 8
VMEM_BYTES = 60 * 1024 * 1024


def shifted(block, axis, distance):
    n = lax.axis_size(axis)
    return lax.ppermute(block, axis, [(i, (i + distance) % n) for i in range(n)])


class Order:
    def __init__(self, mark):
        self.mark = mark

    def __call__(self, *values):
        self.mark, *values = lax.optimization_barrier((self.mark, *values))
        return values


class Ring:
    def __init__(self, block, axis):
        self.axis, self.n, self.step = axis, lax.axis_size(axis), 0
        self.last = (block, block)
        self.up, self.down = [block], []

    def send(self):
        up, down = self.last
        self.step += 1
        if self.step == self.n // 2:
            half = up.shape[0] // 2
            up, down = up[:half], down[half:]
        self.last = (shifted(up, self.axis, -1), shifted(down, self.axis, 1))

    def wait(self, order, *others):
        self.last, *others = order(self.last, *others)
        if self.step < self.n // 2:
            self.up.append(self.last[0])
            self.down.insert(0, self.last[1])
        return others

    def near(self):
        return self.up + self.down


def hidden_kernel(n_rows, *refs):
    rows, tails = refs[:n_rows], refs[n_rows : 2 * n_rows]
    weights = refs[2 * n_rows : -3]
    hidden, route, total = refs[-3:]
    n_experts, n_hid = len(weights), hidden.shape[1]
    step = pl.program_id(0)

    @pl.when(step == 0)
    def _():
        total[...] = jnp.zeros_like(total)
        route[...] = jnp.concatenate([r[...] for r in tails], axis=0)

    x = jnp.concatenate([r[...] for r in rows], axis=0)
    for e in range(n_experts):
        at = slice(2 * n_hid * e, 2 * n_hid * (e + 1))
        total[:, at] += jnp.dot(x, weights[e][0], preferred_element_type=jnp.float32)

    @pl.when(step == pl.num_programs(0) - 1)
    def _():
        named = route[...].astype(jnp.float32)
        gate, up = total[:, :n_hid], total[:, n_hid : 2 * n_hid]
        for e in range(1, n_experts):
            here, at = named == e, 2 * n_hid * e
            gate = jnp.where(here, total[:, at : at + n_hid], gate)
            up = jnp.where(here, total[:, at + n_hid : at + 2 * n_hid], up)
        hidden[...] = (gate / (1.0 + jnp.exp(-gate)) * up).astype(hidden.dtype)


def hidden_of(rows, weights, block):
    n_experts, width, pair = weights.shape
    n_hid = pair // 2
    count = sum(r.shape[0] for r in rows)
    made = jax.ShapeDtypeStruct((count, n_hid), jnp.bfloat16)
    return pl.pallas_call(
        functools.partial(hidden_kernel, len(rows)),
        grid=(width // block,),
        in_specs=[pl.BlockSpec((r.shape[0], block), lambda k: (0, k)) for r in rows]
        + [pl.BlockSpec((r.shape[0], n_hid), lambda k: (0, width // n_hid)) for r in rows]
        + [pl.BlockSpec((1, block, pair), lambda k, e=e: (e, k, 0)) for e in range(n_experts)],
        out_specs=[pl.BlockSpec((count, n_hid), lambda k: (0, 0))] * 2,
        out_shape=[made, made],
        scratch_shapes=[pltpu.VMEM((count, 2 * n_hid * n_experts), jnp.float32)],
        compiler_params=pltpu.CompilerParams(
            dimension_semantics=("arbitrary",), vmem_limit_bytes=VMEM_BYTES
        ),
        cost_estimate=pl.CostEstimate(
            flops=4 * count * width * n_hid * n_experts,
            bytes_accessed=2 * width * (count + 2 * n_hid * n_experts),
            transcendentals=count * n_hid,
        ),
    )(*rows, *rows, *[weights] * n_experts)


def out_kernel(slices, place, route, *refs):
    hidden, weights = refs[:slices], refs[slices:-2]
    out, total = refs[-2:]
    step = pl.program_id(0)
    named = route[...].astype(jnp.float32)

    @pl.when(step == 0)
    def _():
        total[...] = jnp.zeros_like(total)

    for now in range(slices // 2):

        @pl.when(step == now)
        def _():
            sums = total[...]
            for half, weight in zip((hidden[now], hidden[now + slices // 2]), weights):
                n_experts, _, part = weight.shape
                terms = [jnp.where(named == e, half[...], jnp.zeros_like(half)) for e in range(n_experts)]
                sums += jnp.dot(
                    jnp.concatenate(terms, axis=1),
                    weight[...].reshape(-1, part),
                    preferred_element_type=jnp.float32,
                )
            total[...] = sums

    @pl.when(step == pl.num_programs(0) - 1)
    def _():
        out[...] = total[...].astype(out.dtype)


def out_of(place, route, hidden, weights):
    slices = len(hidden)
    n_experts, _, part = weights.shape
    count, n_hid = route.shape
    steps = slices // 2
    return pl.pallas_call(
        functools.partial(out_kernel, slices),
        grid_spec=pltpu.PrefetchScalarGridSpec(
            num_scalar_prefetch=1,
            grid=(steps,),
            in_specs=[pl.BlockSpec((count, n_hid), lambda k, z: (0, 0))]
            + [pl.BlockSpec((count, n_hid), lambda k, z, at=at: (at, 0)) for _, at in hidden]
            + [
                pl.BlockSpec(
                    (n_experts, n_hid, part), lambda k, z, at=at: (0, lax.rem(k + at + z[0], slices), 0)
                )
                for at in (0, steps)
            ],
            out_specs=pl.BlockSpec((count, part), lambda k, z: (0, 0)),
            scratch_shapes=[pltpu.VMEM((count, part), jnp.float32)],
        ),
        out_shape=jax.ShapeDtypeStruct((count, part), jnp.bfloat16),
        compiler_params=pltpu.CompilerParams(
            dimension_semantics=("arbitrary",), vmem_limit_bytes=VMEM_BYTES
        ),
        cost_estimate=pl.CostEstimate(
            flops=2 * count * slices * n_hid * n_experts * part,
            bytes_accessed=2 * slices * n_hid * (count + n_experts * part),
            transcendentals=0,
        ),
    )(place, route, *[h for h, _ in hidden], weights, weights)


def body(
    down_tokens, up_tokens, down_routes, up_routes, down_gates, up_gates, w_gate, w_up, w_down
):
    n_x, n_z = lax.axis_size("x"), lax.axis_size("z")
    me_x, me_z = lax.axis_index("x"), lax.axis_index("z")
    section = lax.axis_index("section")
    sections = lax.axis_size("section")
    even = section % 2 == 0
    rows, width = down_tokens.shape[1:]
    part = width // n_z
    hid = w_gate.shape[2]

    def streams(down, up):
        return jnp.where(even, up, down), jnp.where(even, down, up)

    tokens = streams(down_tokens[0], up_tokens[0])
    gates = streams(down_gates[0], up_gates[0])
    routes = streams(down_routes[0], up_routes[0])

    def marked(s):
        route = jnp.broadcast_to(routes[s].astype(jnp.bfloat16), (rows, hid))
        return jnp.concatenate([tokens[s], route], axis=1)

    def by_place(first, second, s):
        n_first = 2 * (n_z // 2 - 2) + 1
        first = first.reshape(2, n_first, rows, hid)[s]
        second = second.reshape(2, n_z - n_first, rows, hid)[s]
        keep = (n_first + 1) // 2
        turned = jnp.concatenate([first[:keep], second, first[keep:]], axis=0)
        return jnp.roll(turned, me_z, axis=0).reshape(-1, hid)

    def finished(s, out):
        out = out.transpose(1, 0, 2).reshape(rows, width)
        y = tokens[s].astype(jnp.float32) + gates[s] * out.astype(jnp.float32)
        return y.astype(jnp.bfloat16)

    order = Order(gates[0])
    gate_up = lax.all_gather(jnp.concatenate([w_gate[0], w_up[0]], axis=1), "x")
    b, a = Ring(marked(0), "z"), Ring(marked(1), "z")
    b.send()
    a.send()
    w_cut = w_down[0].reshape(hid, n_z, part).transpose(1, 0, 2)
    w_cut = lax.all_to_all(w_cut, "z", 0, 0)
    b.wait(order)
    b.send()
    a.wait(order)
    a.send()
    (w_cut,) = b.wait(order, w_cut)
    b.send()
    down = lax.all_gather(w_cut.reshape(n_z * hid, part), "x")
    a.wait(order)
    first = b.near() + a.near()
    a.send()
    b.wait(order)
    b.send()
    first, first_route = hidden_of(first, gate_up, 1792)
    (first,) = a.wait(order, first)
    a.send()
    b.wait(order)
    a.wait(order)
    second = [p for ring in (b, a) for p in (ring.up[-1], *ring.last, ring.down[0])]
    second, second_route = hidden_of(second, gate_up, 1792)
    both = jnp.concatenate([by_place(first, second, s) for s in range(2)], axis=0)
    named = [by_place(first_route, second_route, s) for s in range(2)]
    h = Ring(both, "z")
    h.send()
    h.wait(order)
    h.send()
    h.wait(order)
    h.send()
    h.wait(order)
    h.send()
    h.wait(order)
    (down,) = order(down)

    def out_rows(s):
        hidden = [(piece, s) for piece in h.up] + [(h.last[s], 0)] + [(piece, s) for piece in h.down]
        return out_of(me_z.astype(jnp.int32).reshape(1), named[s], hidden, down).reshape(n_z, rows, part)

    out_b = lax.all_to_all(out_rows(0), "z", 0, 0)
    out_b, out_a = order(out_b, out_rows(1))
    out_a = lax.all_to_all(out_a, "z", 0, 0)
    gates = (order.mark, gates[1])
    results = [finished(0, out_b), finished(1, out_a)]

    near = [(i, i ^ 1) for i in range(sections)]
    away = [(i, min(max(((i + 1) ^ 1) - 1, 0), sections - 1)) for i in range(sections)]
    from_away = lax.ppermute(results[0], "section", away)
    from_near = lax.ppermute(results[1], "section", near)
    next_down = jnp.where(even, from_away, from_near)
    next_up = jnp.where(even, from_near, from_away)
    return next_down[None], next_up[None]


def solution(mesh):
    sections, devices = mesh.devices.shape
    fine = Mesh(mesh.devices.reshape(sections, devices // SPLIT, SPLIT), ("section", "x", "z"))
    by_rows = P("section", ("x", "z"), None)
    by_columns = P("section", None, ("x", "z"))
    return jax.shard_map(
        body,
        mesh=fine,
        in_specs=(by_rows,) * 6 + (by_columns, by_columns, by_rows),
        out_specs=(by_rows, by_rows),
        check_vma=False,
    )
```
